256 devices in a mesh: turn: 32 (over x, y, core), hist: 8 (over z).
Axes of the slice: x: 4, y: 4, z: 8, core: 2. Of those that a mesh axis runs over, the one named last changes fastest.
Arguments:
- flop_reach: float32 [1326, 128], P(None, 'hist'), may hold values from 0 to 0.01
- turn_policy: int32 [32, 1326, 128], P('turn', None, 'hist'), may hold values from 0 to 256
- river_policy: int32 [32, 5431296], P('turn', 'hist'), may hold values from 0 to 256
- hand_rank: int32 [32, 32, 1326], P('turn', 'hist'), may hold values from 0 to 7461
- turn_cards: int32 [32], P('turn'), may hold values from 3 to 51, as said below
- river_cards: int32 [32, 32], P('turn'), may hold values from 3 to 51, as said below
- children: int32 [64, 2], replicated, may hold values from 0 to 127
- pot: int32 [128], replicated, may hold values from 1 to 24
Outputs:
- turn_value: float32 [32, 84864], P('turn')
- flop_value: float32 [84864], replicated
The draws below stay inside these ranges and needn't reach their ends.
Inputs may be any that keep to these rules, and one draw needn't show every extreme that they name: `turn_cards`: distinct cards, none of the flop cards 0, 1, 2. `river_cards`: for each turn card, distinct cards, none of the flop cards and not that turn card.
All inputs are finite; a program needn't handle non-finite values.
Results may differ from the reference program's by a relative error of at most 0.0003.
Values sent between devices are 32-bit elements; how exact they have to be, the bound alone decides.
No kernel may reach another device: no remote copies, remote signals or barrier semaphores. Data moves between devices by JAX's collectives and lax.ppermute only.
A program may use at most 64 MiB of HBM per device.

```python
import jax
import jax.numpy as jnp
import numpy as np
from jax import lax

H = 1326
HIST = 128
NODES = 64
TURNS = 32
RIVERS = 32


def turn_deck(key):
    middle = jax.random.permutation(key, 47)[:TURNS - 2] + 4
    cards = jnp.concatenate([jnp.array([3, 51], jnp.int32), middle.astype(jnp.int32)])
    order = jax.random.permutation(jax.random.fold_in(key, 5), TURNS)
    return cards[order]


def draw_turn_cards(key, part):
    deck = turn_deck(key)
    return deck.astype(jnp.int32)


def pick_rivers(single, turn_card):
    cards = jnp.arange(48).astype(jnp.int32) + 3
    cards = jnp.where(cards >= turn_card, cards + 1, cards)
    scores = jax.random.permutation(single, 48).astype(jnp.int32) + 2
    scores = jnp.where(cards == 3, 0, scores)
    scores = jnp.where(cards == 51, 1, scores)
    order = jnp.argsort(scores, stable=True)
    return cards[order][:RIVERS]


def draw_river_cards(key, part):
    deck = turn_deck(key)
    key = jax.random.fold_in(key, 7)
    subkeys = jax.random.split(key, TURNS)
    cards = jax.vmap(pick_rivers)(subkeys, deck)
    return cards.astype(jnp.int32)


def plant(drawn, key, least, top_value):
    longest = drawn.shape.index(max(drawn.shape))
    spots = []
    for shift in (0, 1):
        where = [jax.random.randint(jax.random.fold_in(key, axis), (), 0, length) for axis, length in enumerate(drawn.shape)]
        where[longest] = (where[longest] + shift) % drawn.shape[longest]
        spots.append(tuple(where))
    return drawn.at[spots[0]].set(least).at[spots[1]].set(top_value)


def steps_of(rng, extent, cuts, least, top_value):
    loudness = 1.0
    for axis_at, shards_of in cuts:
        heights = jax.random.uniform(jax.random.fold_in(jax.random.fold_in(rng, 6), axis_at), (shards_of,), jnp.float32, least / len(cuts), top_value / len(cuts))
        loudness = loudness * jnp.repeat(jnp.exp(heights), extent[axis_at] // shards_of).reshape((-1,) + (1,) * (len(extent) - 1 - axis_at))
    return loudness


def setup_inputs(seed: int = 0) -> dict:
    key_of = jax.random.split(jax.random.key(seed), 9)
    flop_reach = jnp.clip(0.01 * jax.random.uniform(key_of[0], (H, HIST), jnp.float32) ** steps_of(key_of[0], (H, HIST), ((1, 8),), -0.2, 0.2), 0.0, 0.01)
    turn_policy = plant(jax.random.randint(key_of[1], (TURNS, H, HIST), 0, 257), jax.random.fold_in(key_of[1], 1), 0, 256).astype(jnp.int32)
    river_policy = plant(jax.random.randint(key_of[2], (TURNS, HIST * RIVERS * H), 0, 257), jax.random.fold_in(key_of[2], 1), 0, 256).astype(jnp.int32)
    hand_rank = plant(jax.random.randint(key_of[3], (TURNS, RIVERS, H), 0, 7462), jax.random.fold_in(key_of[3], 1), 0, 7461).astype(jnp.int32)
    turn_cards = draw_turn_cards(jax.random.fold_in(key_of[8], 71), 0)
    river_cards = draw_river_cards(jax.random.fold_in(key_of[8], 71), 0)
    children = plant(jax.random.randint(key_of[6], (NODES, 2), 0, HIST), jax.random.fold_in(key_of[6], 1), 0, HIST - 1).astype(jnp.int32)
    pot = plant(jax.random.randint(key_of[7], (HIST,), 1, 25), jax.random.fold_in(key_of[7], 1), 1, 24).astype(jnp.int32)
    return {"flop_reach": flop_reach, "turn_policy": turn_policy, "river_policy": river_policy, "hand_rank": hand_rank, "turn_cards": turn_cards, "river_cards": river_cards, "children": children, "pot": pot}


def hand_cards():
    first, second = np.triu_indices(52, 1)
    return jnp.asarray(first, jnp.int32), jnp.asarray(second, jnp.int32)


def not_holding(first, second, card):
    return (first != card) & (second != card)


def showdown(reach, ranks, livef, compat, potf):
    wins = jnp.sign(ranks[:, None] - ranks[None, :]).astype(jnp.float32)
    payoff = wins * compat
    value = jnp.dot(payoff, reach, precision=lax.Precision.HIGHEST, preferred_element_type=jnp.float32)
    return value * potf[None, :] * livef[:, None]


def best_reply(value, children):
    return jnp.maximum(value[:, children[:, 0]], value[:, children[:, 1]])


def reference(flop_reach, turn_policy, river_policy, hand_rank, turn_cards, river_cards, children, pot):
    first, second = hand_cards()
    flop_live = not_holding(first, second, 0) & not_holding(first, second, 1) & not_holding(first, second, 2)
    compat = ((first[:, None] != first[None, :]) & (first[:, None] != second[None, :])
              & (second[:, None] != first[None, :]) & (second[:, None] != second[None, :])).astype(jnp.float32)
    potf = pot.astype(jnp.float32)

    def per_turn(index):
        turn_live = flop_live & not_holding(first, second, turn_cards[index])
        reach_turn = flop_reach * (turn_policy[index].astype(jnp.float32) / 256.0) * turn_live[:, None].astype(jnp.float32)
        policy_all = river_policy[index].reshape(HIST, RIVERS, H)

        def per_river(river):
            live = turn_live & not_holding(first, second, river_cards[index, river])
            livef = live.astype(jnp.float32)
            policy = jnp.transpose(policy_all[:, river, :]).astype(jnp.float32)
            reach_river = reach_turn * (policy / 256.0) * livef[:, None]
            value = showdown(reach_river, hand_rank[index, river], livef, compat, potf)
            return best_reply(value, children)

        replies = lax.map(per_river, jnp.arange(RIVERS).astype(jnp.int32))
        total = jnp.sum(replies, axis=0) / RIVERS
        return jnp.transpose(total).reshape(-1)

    turn_value = lax.map(per_turn, jnp.arange(TURNS).astype(jnp.int32))
    flop_value = jnp.sum(turn_value, axis=0) / TURNS
    return turn_value, flop_value
```

```python
import functools

import jax
import jax.numpy as jnp
import numpy as np
from jax import lax
from jax.experimental import pallas as pl
from jax.experimental.pallas import tpu as pltpu
from jax.sharding import PartitionSpec as P

HANDS = 1326
LOW = 150
BASE = 245
SLOTS = HANDS - BASE
TILES = 9
WIDE = TILES * 128
ROWS = 17
VMEM_LIMIT = 56 * 1024 * 1024


def slot_cards():
    first, second = np.triu_indices(52, 1)
    a = np.full((WIDE,), 200, np.int32)
    b = np.full((WIDE,), 201, np.int32)
    a[:SLOTS], b[:SLOTS] = first[BASE:], second[BASE:]
    return a, b


def compat_table():
    a, b = slot_cards()
    real = np.arange(WIDE) < SLOTS
    shares = (
        (a[:, None] == a[None, :])
        | (a[:, None] == b[None, :])
        | (b[:, None] == a[None, :])
        | (b[:, None] == b[None, :])
    )
    return (~shares & real[:, None] & real[None, :]).astype(np.float32)


def renamed(t, r):
    return jnp.where(r == 3, 4, 3), jnp.where(t == 4, 3, 4)


def source_lanes(a, b, t, r):
    card_t, card_r = renamed(t, r)
    off_t = jnp.where(card_t == 3, -4, 43)
    off_r = jnp.where(card_r == 3, -4, 43)
    has_t = (a == t) | (b == t)
    has_r = (a == r) | (b == r)
    from_t = jnp.where(a == t, b, a) + off_t
    from_r = jnp.where(a == r, b, a) + off_r
    one = jnp.where(has_t, from_t, jnp.where(has_r, from_r, -1))
    return jnp.where(has_t & has_r, 0, one)


def home_slots(lane, t, r):
    card_t, card_r = renamed(t, r)
    t_high, r_high = t >= 5, r >= 5
    none = jnp.int32(-1)
    name3 = jnp.where(t_high & (card_t == 3), t, jnp.where(r_high & (card_r == 3), r, none))
    name4 = jnp.where(t_high & (card_t == 4), t, jnp.where(r_high & (card_r == 4), r, none))
    of3 = lane < 48
    x = jnp.where(of3, lane + 4, lane - 43)
    p = jnp.where(of3, name3, name4)
    q = jnp.where(x == 4, name4, x)
    good = (lane < 95) & (p >= 5) & (q >= 5) & (x != t) & (x != r)
    low, high = jnp.minimum(p, q), jnp.maximum(p, q)
    u = low - 5
    slot = u * 46 - ((u * (u - 1)) >> 1) + high - low - 1
    return jnp.where(good, slot, -1)


def lanes_of(shape):
    return lax.broadcasted_iota(jnp.int32, shape, 1)


def pick(values, index):
    return jnp.take_along_axis(values, index, axis=1, mode="promise_in_bounds")


def tile(ref, j):
    return ref[:, 128 * j : 128 * j + 128]


def pack_kernel(scal, policy, flop_reach, turn_policy, slot_a, slot_b, *rest):
    outs, (raw, own, low) = rest[:8], rest[8:]
    me, t = scal[0], scal[1]
    lane = lanes_of((8, 128))
    reach = flop_reach[...] * (turn_policy[...].astype(jnp.float32) * (1.0 / 256.0)) * (1.0 / 256.0)
    reach = jnp.concatenate([reach, jnp.zeros((16, 1408 - HANDS), jnp.float32)], axis=1)
    for j in range(11):
        raw[16 * j : 16 * j + 16, :] = reach[:, 128 * j : 128 * j + 128]
    wide = lanes_of((8, 1408))
    for p in range(2):
        reach = jnp.concatenate([raw[pl.ds(16 * j + p, 8, stride=2), :] for j in range(11)], axis=1)
        moved = pltpu.roll(reach, 1408 - BASE, 1)
        own[p] = jnp.where(wide < SLOTS, moved, 0.0)[:, :WIDE]
        moved = pltpu.roll(reach, 1408 - LOW, 1)
        low[p] = jnp.where(wide < 95, moved, 0.0)[:, :128]

    def one_river(out, rl, river):
        r = scal[2 + river]
        index = [source_lanes(tile(slot_a, j), tile(slot_b, j), t, r) for j in range(TILES)]
        tails = []
        for p in range(2):

            def aligned(start, count):
                row, shift = start >> 7, start & 127
                turn = (128 - shift) & 127
                rolled = [
                    pltpu.roll(policy[pl.ds(jnp.minimum(row + i, 662), 8, stride=663), :], turn, 1)
                    for i in range(count + 1)
                ]
                keep = lane < 128 - shift
                return [
                    jnp.where(keep, rolled[i], rolled[i + 1]).astype(jnp.float32) for i in range(count)
                ]

            start = p * 42432 + river * HANDS + LOW
            source = aligned(start, 1)[0] * low[p]
            plain = aligned(start + (BASE - LOW), TILES)
            for j in range(TILES):
                kept = plain[j] * own[p, :, 128 * j : 128 * j + 128]
                taken = pick(source, jnp.maximum(index[j], 0))
                value = jnp.where(index[j] >= 0, taken, kept)
                if j < 8:
                    out[rl, 8 * p + j] = value
                else:
                    tails.append(value)
        out[rl, 16] = tails[0] + pltpu.roll(tails[1], 64, 1)

    for s in range(8):
        group = (me + s) & 7

        @pl.loop(0, 4)
        def _(rl, out=outs[s], group=group):
            one_river(out, rl, group * 4 + rl)


def pack(scal, policy, flop_reach, turn_policy, slot_a, slot_b):
    smem = pl.BlockSpec(memory_space=pltpu.SMEM)
    vmem = pl.BlockSpec(memory_space=pltpu.VMEM)
    return pl.pallas_call(
        pack_kernel,
        out_shape=[jax.ShapeDtypeStruct((4, ROWS, 8, 128), jnp.float32)] * 8,
        in_specs=[smem] + [vmem] * 5,
        out_specs=[vmem] * 8,
        scratch_shapes=[
            pltpu.VMEM((176, 128), jnp.float32),
            pltpu.VMEM((2, 8, WIDE), jnp.float32),
            pltpu.VMEM((2, 8, 128), jnp.float32),
        ],
        compiler_params=pltpu.CompilerParams(vmem_limit_bytes=VMEM_LIMIT),
        name="pack",
    )(scal, policy, flop_reach, turn_policy, slot_a, slot_b)


def payoff_kernel(scal, ranks, compat, slot_a, slot_b, out, rows, strip):
    rl = pl.program_id(0)
    t = scal[1]
    r = scal[2 + 4 * scal[0] + rl]
    raw = ranks[...]
    value = (128 + (raw & 127)).astype(jnp.float32)
    for bit in range(6):
        value = value * jnp.where(((raw >> (7 + bit)) & 1) == 1, float(2 ** (2**bit)), 1.0)
    rows[...] = jnp.zeros_like(rows)
    rows[0:4, :HANDS] = value
    row = jnp.broadcast_to(rows[pl.ds(rl, 1), :], (8, 1408))
    plain = pltpu.roll(row, 1408 - BASE, 1)
    source = pltpu.roll(row, 1408 - LOW, 1)[:, :128]
    for j in range(TILES):
        index = source_lanes(tile(slot_a, j), tile(slot_b, j), t, r)
        taken = pick(source, jnp.maximum(index, 0))
        strip[:, 128 * j : 128 * j + 128] = jnp.where(index >= 0, taken, plain[:, 128 * j : 128 * j + 128])
    across = [
        jnp.broadcast_to(strip[0:1, 128 * j : 128 * j + 128], (128, 128)).astype(jnp.bfloat16)
        for j in range(TILES)
    ]
    for i in range(TILES):
        down = jnp.transpose(jnp.broadcast_to(strip[0:1, 128 * i : 128 * i + 128], (128, 128)))
        down = down.astype(jnp.bfloat16)
        for j in range(TILES):
            mask = compat[128 * i : 128 * i + 128, 128 * j : 128 * j + 128]
            out[0, 128 * i : 128 * i + 128, 128 * j : 128 * j + 128] = jnp.minimum(
                jnp.maximum(across[j] - down, -mask), mask
            )


def payoffs(scal, ranks, compat, slot_a, slot_b):
    smem = pl.BlockSpec(memory_space=pltpu.SMEM)
    vmem = pl.BlockSpec(memory_space=pltpu.VMEM)
    return pl.pallas_call(
        payoff_kernel,
        grid=(4,),
        out_shape=jax.ShapeDtypeStruct((4, WIDE, WIDE), jnp.bfloat16),
        in_specs=[smem] + [vmem] * 4,
        out_specs=pl.BlockSpec((1, WIDE, WIDE), lambda i: (i, 0, 0)),
        scratch_shapes=[pltpu.VMEM((8, 1408), jnp.float32), pltpu.VMEM((8, WIDE), jnp.float32)],
        compiler_params=pltpu.CompilerParams(vmem_limit_bytes=VMEM_LIMIT),
        cost_estimate=pl.CostEstimate(flops=4 * 4 * WIDE * WIDE, bytes_accessed=10 * WIDE * WIDE, transcendentals=0),
        name="payoff",
    )(scal, ranks, compat, slot_a, slot_b)


def reply_kernel(scal, payoff, select, scale, slot_a, slot_b, *rest):
    blocks, out, high, rest_low = rest[:8], rest[8], rest[9], rest[10]
    rl = pl.program_id(0)
    t = scal[1]
    r = scal[2 + 4 * scal[0] + rl]
    lane = lanes_of((8, 128))
    for s in range(8):
        for j in range(TILES):
            if j < 8:
                pair = [blocks[s][0, j], blocks[s][0, 8 + j]]
            else:
                tails = blocks[s][0, 16]
                pair = [jnp.where(lane < 64, v, 0.0) for v in (tails, pltpu.roll(tails, 64, 1))]
            both = jnp.concatenate(pair, axis=0)
            upper = both.astype(jnp.bfloat16)
            high[16 * s : 16 * s + 16, 128 * j : 128 * j + 128] = upper
            rest_low[16 * s : 16 * s + 16, 128 * j : 128 * j + 128] = (
                both - upper.astype(jnp.float32)
            ).astype(jnp.bfloat16)
    dot = functools.partial(jnp.dot, preferred_element_type=jnp.float32)
    chosen = jnp.concatenate(
        [dot(select[...], high[...]).astype(jnp.bfloat16), dot(select[...], rest_low[...]).astype(jnp.bfloat16)],
        axis=0,
    )
    value = dot(chosen, payoff[0])
    value = (value[:128] + value[128:]) * scale[...]
    reply = jnp.maximum(value[:64], value[64:])

    @pl.when(rl == 0)
    def _():
        out[...] = jnp.zeros_like(out)

    home = home_slots(lane, t, r)
    for j in range(TILES):
        moved = source_lanes(tile(slot_a, j), tile(slot_b, j), t, r) >= 0
        for g in range(8):
            part = reply[8 * g : 8 * g + 8, 128 * j : 128 * j + 128]
            out[g, 1 + j] += jnp.where(moved, 0.0, part)
            out[g, 0] += jnp.where((home >> 7) == j, pick(part, home & 127), 0.0)


def replies(scal, payoff, select, scale, slot_a, slot_b, blocks):
    smem = pl.BlockSpec(memory_space=pltpu.SMEM)
    vmem = pl.BlockSpec(memory_space=pltpu.VMEM)
    block = pl.BlockSpec((1, ROWS, 8, 128), lambda i: (i, 0, 0, 0))
    return pl.pallas_call(
        reply_kernel,
        grid=(4,),
        out_shape=jax.ShapeDtypeStruct((8, TILES + 1, 8, 128), jnp.float32),
        in_specs=[smem, pl.BlockSpec((1, WIDE, WIDE), lambda i: (i, 0, 0))] + [vmem] * 4 + [block] * 8,
        out_specs=vmem,
        scratch_shapes=[pltpu.VMEM((128, WIDE), jnp.bfloat16)] * 2,
        compiler_params=pltpu.CompilerParams(vmem_limit_bytes=VMEM_LIMIT),
        cost_estimate=pl.CostEstimate(
            flops=4 * 2 * 256 * WIDE * WIDE, bytes_accessed=8 * WIDE * WIDE, transcendentals=0
        ),
        name="reply",
    )(scal, payoff, select, scale, slot_a, slot_b, *blocks)


def flat(nodes):
    rows = jnp.transpose(nodes, (0, 2, 1, 3)).reshape(64, TILES + 1, 128)
    body = rows[:, 1:].reshape(64, WIDE)[:, :SLOTS]
    return jnp.concatenate([jnp.zeros((64, LOW), jnp.float32), rows[:, 0, :95], body], axis=1).reshape(-1)


def turn_sum(value, size):
    bit = 1
    while bit < size:
        value = value + lax.ppermute(value, "turn", [(i, i ^ bit) for i in range(size)])
        bit *= 2
    return value


def per_device(flop_reach, turn_policy, river_policy, hand_rank, turn_cards, river_cards, children, pot):
    groups = lax.axis_size("hist")
    turns = lax.axis_size("turn")
    me = lax.axis_index("hist")
    a, b = slot_cards()
    slot_a = jnp.asarray(np.broadcast_to(a, (8, WIDE)))
    slot_b = jnp.asarray(np.broadcast_to(b, (8, WIDE)))
    compat = jnp.asarray(compat_table(), jnp.bfloat16)
    scal = jnp.concatenate([me.reshape(1).astype(jnp.int32), turn_cards, river_cards[0]])
    packed = pack(
        scal,
        river_policy.reshape(5304, 128),
        jnp.transpose(flop_reach),
        jnp.transpose(turn_policy[0]),
        slot_a,
        slot_b,
    )
    blocks = [packed[0]]
    for s in range(1, groups):
        blocks.append(lax.ppermute(packed[s], "hist", [(i, (i + s) % groups) for i in range(groups)]))
    payoff = payoffs(scal, hand_rank[0], compat, slot_a, slot_b)
    child = jnp.transpose(children).reshape(128)
    place = (((me - (child >> 4)) & 7) << 4) + ((child & 1) << 3) + ((child >> 1) & 7)
    select = (place[:, None] == jnp.arange(128)[None, :]).astype(jnp.bfloat16)
    scale = jnp.sum(
        jnp.where(child[:, None] == jnp.arange(128)[None, :], pot.astype(jnp.float32)[None, :], 0.0),
        axis=1,
        keepdims=True,
    )
    partial = replies(scal, payoff, select, scale, slot_a, slot_b, blocks)
    arrived = lax.all_to_all(partial, "hist", 0, 0, tiled=True)
    value = jnp.sum(arrived, axis=0) * (1.0 / 32.0)
    mean = turn_sum(value, turns) * (1.0 / turns)
    both = jnp.stack([value, mean])
    spread = lax.all_to_all(jnp.broadcast_to(both, (groups,) + both.shape), "hist", 0, 0, tiled=True)
    return (flat(spread[:, 0]).reshape(1, -1), flat(spread[:, 1]))


def solution(mesh):
    return jax.shard_map(
        per_device,
        mesh=mesh,
        in_specs=(
            P(None, "hist"),
            P("turn", None, "hist"),
            P("turn", "hist"),
            P("turn", "hist", None),
            P("turn"),
            P("turn", None),
            P(),
            P(),
        ),
        out_specs=(P("turn", None), P()),
        check_vma=False,
    )
```

```python
import functools

import jax
import jax.numpy as jnp
import numpy as np
from jax import lax
from jax.experimental import pallas as pl
from jax.experimental.pallas import tpu as pltpu
from jax.sharding import PartitionSpec as P

HANDS = 1326
LOW = 150
BASE = 245
SLOTS = HANDS - BASE
TILES = 9
WIDE = TILES * 128
ROWS = 17
ORDER = (4, 3, 5, 2, 6, 1, 7, 0)
CHUNK = 256
VMEM_LIMIT = 56 * 1024 * 1024


def slot_cards():
    first, second = np.triu_indices(52, 1)
    a = np.full((WIDE,), 200, np.int32)
    b = np.full((WIDE,), 201, np.int32)
    a[:SLOTS], b[:SLOTS] = first[BASE:], second[BASE:]
    return a, b


def compat_table():
    a, b = slot_cards()
    real = np.arange(WIDE) < SLOTS
    shares = (
        (a[:, None] == a[None, :])
        | (a[:, None] == b[None, :])
        | (b[:, None] == a[None, :])
        | (b[:, None] == b[None, :])
    )
    return (~shares & real[:, None] & real[None, :]).astype(np.float32)


def renamed(t, r):
    return jnp.where(r == 3, 4, 3), jnp.where(t == 4, 3, 4)


def source_lanes(a, b, t, r):
    card_t, card_r = renamed(t, r)
    off_t = jnp.where(card_t == 3, -4, 43)
    off_r = jnp.where(card_r == 3, -4, 43)
    has_t = (a == t) | (b == t)
    has_r = (a == r) | (b == r)
    from_t = jnp.where(a == t, b, a) + off_t
    from_r = jnp.where(a == r, b, a) + off_r
    one = jnp.where(has_t, from_t, jnp.where(has_r, from_r, -1))
    return jnp.where(has_t & has_r, 0, one)


def home_slots(lane, t, r):
    card_t, card_r = renamed(t, r)
    t_high, r_high = t >= 5, r >= 5
    none = jnp.int32(-1)
    name3 = jnp.where(t_high & (card_t == 3), t, jnp.where(r_high & (card_r == 3), r, none))
    name4 = jnp.where(t_high & (card_t == 4), t, jnp.where(r_high & (card_r == 4), r, none))
    of3 = lane < 48
    x = jnp.where(of3, lane + 4, lane - 43)
    p = jnp.where(of3, name3, name4)
    q = jnp.where(x == 4, name4, x)
    good = (lane < 95) & (p >= 5) & (q >= 5) & (x != t) & (x != r)
    low, high = jnp.minimum(p, q), jnp.maximum(p, q)
    u = low - 5
    slot = u * 46 - ((u * (u - 1)) >> 1) + high - low - 1
    return jnp.where(good, slot, -1)


def lanes_of(shape):
    return lax.broadcasted_iota(jnp.int32, shape, 1)


def pick(values, index):
    return jnp.take_along_axis(values, index, axis=1, mode="promise_in_bounds")


def tile(ref, j):
    return ref[:, 128 * j : 128 * j + 128]


def cards_of(table, j):
    return [jnp.broadcast_to(table[i : i + 1, 128 * j : 128 * j + 128], (8, 128)) for i in range(2)]


def pack_kernel(first, turn_card, river_card, policy_hbm, flop_reach, turn_policy, table, *rest):
    outs, (policy, staged, raw, own, low, in_sem, out_sem) = (rest[:1] if first else rest[1:8]), rest[-7:]
    fetch = pltpu.make_async_copy(policy_hbm, policy, in_sem)
    fetch.start()
    me, t = lax.axis_index("hist"), turn_card[0]
    lane = lanes_of((8, 128))
    reach = flop_reach[...] * (turn_policy[...].astype(jnp.float32) * (1.0 / 256.0)) * (1.0 / 256.0)
    reach = jnp.concatenate([reach, jnp.zeros((16, 1408 - HANDS), jnp.float32)], axis=1)
    for j in range(11):
        raw[16 * j : 16 * j + 16, :] = reach[:, 128 * j : 128 * j + 128]
    wide = lanes_of((8, 1408))
    for p in range(2):
        reach = jnp.concatenate([raw[pl.ds(16 * j + p, 8, stride=2), :] for j in range(11)], axis=1)
        moved = pltpu.roll(reach, 1408 - BASE, 1)
        own[p] = jnp.where(wide < SLOTS, moved, 0.0)[:, :WIDE]
        moved = pltpu.roll(reach, 1408 - LOW, 1)
        low[p] = jnp.where(wide < 95, moved, 0.0)[:, :128]

    def one_river(out, rl, river):
        r = river_card[0, river]
        index = [source_lanes(*cards_of(table, j), t, r) for j in range(TILES)]
        tails = []
        for p in range(2):

            def aligned(start, count):
                row, shift = start >> 7, start & 127
                turn = (128 - shift) & 127
                rolled = [
                    pltpu.roll(policy[pl.ds(jnp.minimum(row + i, 662), 8, stride=663), :], turn, 1)
                    for i in range(count + 1)
                ]
                keep = lane < 128 - shift
                return [
                    jnp.where(keep, rolled[i], rolled[i + 1]).astype(jnp.float32) for i in range(count)
                ]

            start = p * 42432 + river * HANDS + LOW
            source = aligned(start, 1)[0] * low[p]
            plain = aligned(start + (BASE - LOW), TILES)
            for j in range(TILES):
                kept = plain[j] * own[p, :, 128 * j : 128 * j + 128]
                taken = pick(source, jnp.maximum(index[j], 0))
                value = jnp.where(index[j] >= 0, taken, kept)
                if j < 8:
                    out[rl, 8 * p + j] = value
                else:
                    tails.append(value)
        out[rl, 16] = tails[0] + pltpu.roll(tails[1], 64, 1)

    fetch.wait()
    stores = [pltpu.make_async_copy(staged.at[i], out, out_sem.at[i]) for i, out in enumerate(outs)]

    @pl.loop(0, 2 * len(outs))
    def _(step):
        i, rl = step >> 1, 2 * (step & 1)
        shift = 4 if first else jnp.where((i & 1) == 1, 5 + (i >> 1), 3 - (i >> 1))
        river = ((me + shift) & 7) * 4 + rl
        one_river(staged.at[i], rl, river)
        one_river(staged.at[i], rl + 1, river + 1)
        for k, store in enumerate(stores):

            @pl.when(step == 2 * k + 1)
            def _(store=store):
                store.start()

    for store in stores:
        store.wait()


def pack(turn_cards, river_cards, policy, flop_reach, turn_policy, table, after):
    count = 7 if after else 1
    smem = pl.BlockSpec(memory_space=pltpu.SMEM)
    vmem = pl.BlockSpec(memory_space=pltpu.VMEM)
    anywhere = pl.BlockSpec(memory_space=pl.ANY)
    message = (4, ROWS, 8, 128)
    return pl.pallas_call(
        functools.partial(pack_kernel, not after),
        out_shape=[jax.ShapeDtypeStruct(message, jnp.float32)] * count,
        in_specs=[smem] * 2 + [anywhere] + [vmem] * 3 + [anywhere] * len(after),
        out_specs=[anywhere] * count,
        scratch_shapes=[
            pltpu.VMEM((5304, 128), jnp.int32),
            pltpu.VMEM((count,) + message, jnp.float32),
            pltpu.VMEM((176, 128), jnp.float32),
            pltpu.VMEM((2, 8, WIDE), jnp.float32),
            pltpu.VMEM((2, 8, 128), jnp.float32),
            pltpu.SemaphoreType.DMA,
            pltpu.SemaphoreType.DMA((count,)),
        ],
        compiler_params=pltpu.CompilerParams(vmem_limit_bytes=VMEM_LIMIT),
        cost_estimate=pl.CostEstimate(flops=3000000, bytes_accessed=4000000, transcendentals=0),
        name="pack",
    )(turn_cards, river_cards, policy, flop_reach, turn_policy, table, *after)


def payoff_kernel(turn_card, river_card, ranks, compat, table, after, out, rows, strip):
    rl = pl.program_id(0)
    t = turn_card[0]
    r = river_card[0, 4 * lax.axis_index("hist") + rl]
    raw = ranks[...]
    value = (128 + (raw & 127)).astype(jnp.float32)
    for bit in range(6):
        value = value * jnp.where(((raw >> (7 + bit)) & 1) == 1, float(2 ** (2**bit)), 1.0)
    rows[...] = jnp.zeros_like(rows)
    rows[0:4, :HANDS] = value
    row = jnp.broadcast_to(rows[pl.ds(rl, 1), :], (8, 1408))
    plain = pltpu.roll(row, 1408 - BASE, 1)
    source = pltpu.roll(row, 1408 - LOW, 1)[:, :128]
    for j in range(TILES):
        index = source_lanes(*cards_of(table, j), t, r)
        taken = pick(source, jnp.maximum(index, 0))
        strip[:, 128 * j : 128 * j + 128] = jnp.where(index >= 0, taken, plain[:, 128 * j : 128 * j + 128])
    across = [
        jnp.broadcast_to(strip[0:1, 128 * j : 128 * j + 128], (128, 128)).astype(jnp.bfloat16)
        for j in range(TILES)
    ]
    code = jnp.where(lax.broadcasted_iota(jnp.int32, (8, WIDE), 0) == 0, strip[...], 0.0).astype(jnp.bfloat16)
    column = lax.dot_general(
        code, jnp.ones((8, 128), jnp.bfloat16), (((0,), (0,)), ((), ())), preferred_element_type=jnp.float32
    ).astype(jnp.bfloat16)
    for i in range(TILES):
        down = column[128 * i : 128 * i + 128]
        for j in range(TILES):
            mask = compat[128 * i : 128 * i + 128, 128 * j : 128 * j + 128]
            out[0, 128 * i : 128 * i + 128, 128 * j : 128 * j + 128] = jnp.minimum(
                jnp.maximum(across[j] - down, -mask), mask
            )


def payoffs(turn_cards, river_cards, ranks, compat, table, after):
    smem = pl.BlockSpec(memory_space=pltpu.SMEM)
    vmem = pl.BlockSpec(memory_space=pltpu.VMEM)
    return pl.pallas_call(
        payoff_kernel,
        grid=(4,),
        out_shape=jax.ShapeDtypeStruct((4, WIDE, WIDE), jnp.bfloat16),
        in_specs=[smem] * 2 + [vmem] * 3 + [pl.BlockSpec(memory_space=pl.ANY)],
        out_specs=pl.BlockSpec((1, WIDE, WIDE), lambda i: (i, 0, 0)),
        scratch_shapes=[pltpu.VMEM((8, 1408), jnp.float32), pltpu.VMEM((8, WIDE), jnp.float32)],
        compiler_params=pltpu.CompilerParams(vmem_limit_bytes=VMEM_LIMIT),
        cost_estimate=pl.CostEstimate(flops=4 * 4 * WIDE * WIDE, bytes_accessed=10 * WIDE * WIDE, transcendentals=0),
        name="payoff",
    )(turn_cards, river_cards, ranks, compat, table, after)


def reply_kernel(turn_card, river_card, payoff, select, scale, table, *rest):
    blocks, (out, high, fine) = rest[:8], rest[8:]
    rl = pl.program_id(0)
    t = turn_card[0]
    r = river_card[0, 4 * lax.axis_index("hist") + rl]
    lane = lanes_of((8, 128))
    for s in range(8):
        for j in range(TILES):
            if j < 8:
                pair = [blocks[s][0, j], blocks[s][0, 8 + j]]
            else:
                tails = blocks[s][0, 16]
                pair = [jnp.where(lane < 64, v, 0.0) for v in (tails, pltpu.roll(tails, 64, 1))]
            both = jnp.concatenate(pair, axis=0)
            upper = both.astype(jnp.bfloat16)
            high[16 * s : 16 * s + 16, 128 * j : 128 * j + 128] = upper
            fine[16 * s : 16 * s + 16, 128 * j : 128 * j + 128] = (
                both - upper.astype(jnp.float32)
            ).astype(jnp.bfloat16)
    dot = functools.partial(jnp.dot, preferred_element_type=jnp.float32)
    chosen = jnp.concatenate(
        [dot(select[...], high[...]).astype(jnp.bfloat16), dot(select[...], fine[...]).astype(jnp.bfloat16)],
        axis=0,
    )

    @pl.when(rl == 0)
    def _():
        out[...] = jnp.zeros_like(out)

    home = home_slots(lane, t, r)
    home_tile, home_lane = home >> 7, home & 127
    first = [jnp.zeros((8, 128), jnp.float32)] * 8
    for start in range(0, WIDE, CHUNK):
        value = dot(chosen, payoff[0, :, start : start + CHUNK])
        value = (value[:128] + value[128:]) * scale[...]
        reply = jnp.maximum(value[:64], value[64:])
        for j in range(start // 128, min(start + CHUNK, WIDE) // 128):
            moved = source_lanes(*cards_of(table, j), t, r) >= 0
            for g in range(8):
                part = reply[8 * g : 8 * g + 8, 128 * j - start : 128 * j - start + 128]
                out[g, 1 + j] += jnp.where(moved, 0.0, part)
                first[g] = jnp.where(home_tile == j, pick(part, home_lane), first[g])
    for g in range(8):
        out[g, 0] += first[g]


def replies(turn_cards, river_cards, payoff, select, scale, table, blocks):
    smem = pl.BlockSpec(memory_space=pltpu.SMEM)
    vmem = pl.BlockSpec(memory_space=pltpu.VMEM)
    return pl.pallas_call(
        reply_kernel,
        grid=(4,),
        out_shape=jax.ShapeDtypeStruct((8, TILES + 1, 8, 128), jnp.float32),
        in_specs=[smem] * 2
        + [pl.BlockSpec((1, WIDE, WIDE), lambda i: (i, 0, 0))]
        + [vmem] * 3
        + [pl.BlockSpec((1, ROWS, 8, 128), lambda i: (i, 0, 0, 0))] * 8,
        out_specs=vmem,
        scratch_shapes=[pltpu.VMEM((128, WIDE), jnp.bfloat16)] * 2,
        compiler_params=pltpu.CompilerParams(vmem_limit_bytes=VMEM_LIMIT),
        cost_estimate=pl.CostEstimate(
            flops=4 * 2 * 256 * WIDE * WIDE, bytes_accessed=8 * WIDE * WIDE, transcendentals=0
        ),
        name="reply",
    )(turn_cards, river_cards, payoff, select, scale, table, *blocks)


def flat(nodes):
    rows = jnp.transpose(nodes, (0, 2, 1, 3)).reshape(64, TILES + 1, 128)
    body = rows[:, 1:].reshape(64, WIDE)[:, :SLOTS]
    return jnp.concatenate([jnp.zeros((64, LOW), jnp.float32), rows[:, 0, :95], body], axis=1).reshape(-1)


def turn_sum(value, size):
    value = value + lax.ppermute(value, "turn", [(i, i ^ 1) for i in range(size)])
    step = 2
    while step < size:
        near = [
            lax.ppermute(
                value,
                "turn",
                [(i, i - i % (4 * step) + (i + s * step) % (4 * step)) for i in range(size)],
            )
            for s in (1, 2, 3)
        ]
        value = (value + near[1]) + (near[0] + near[2])
        step *= 4
    return value


def per_device(flop_reach, turn_policy, river_policy, hand_rank, turn_cards, river_cards, children, pot):
    groups = lax.axis_size("hist")
    turns = lax.axis_size("turn")
    me = lax.axis_index("hist")
    table = jnp.asarray(np.stack(slot_cards()))
    compat = jnp.asarray(compat_table(), jnp.bfloat16)
    policy = river_policy.reshape(5304, 128)
    common = (turn_cards, river_cards, policy, jnp.transpose(flop_reach), jnp.transpose(turn_policy[0]), table)

    def send(block, s):
        return lax.ppermute(block, "hist", [(i, (i + s) % groups) for i in range(groups)])

    packed = pack(*common, [])
    packed += pack(*common, packed)
    got = [send(block, s) if s else block for block, s in zip(packed, ORDER)]
    payoff = payoffs(turn_cards, river_cards, hand_rank[0], compat, table, packed[1])
    child = jnp.transpose(children).reshape(128)
    turn_of = jnp.zeros((8,), jnp.int32).at[jnp.array(ORDER)].set(jnp.arange(8, dtype=jnp.int32))
    place = (turn_of[(me - (child >> 4)) & 7] << 4) + ((child & 1) << 3) + ((child >> 1) & 7)
    select = (place[:, None] == jnp.arange(128)[None, :]).astype(jnp.bfloat16)
    scale = jnp.sum(
        jnp.where(child[:, None] == jnp.arange(128)[None, :], pot.astype(jnp.float32)[None, :], 0.0),
        axis=1,
        keepdims=True,
    )
    partial = replies(turn_cards, river_cards, payoff, select, scale, table, got)
    arrived = lax.all_to_all(partial, "hist", 0, 0, tiled=True)
    value = jnp.sum(arrived, axis=0) * (1.0 / 32.0)
    mean = turn_sum(value, turns) * (1.0 / turns)
    both = jnp.stack([value, mean])
    spread = lax.all_to_all(jnp.broadcast_to(both, (groups,) + both.shape), "hist", 0, 0, tiled=True)
    return (flat(spread[:, 0]).reshape(1, -1), flat(spread[:, 1]))


def solution(mesh):
    return jax.shard_map(
        per_device,
        mesh=mesh,
        in_specs=(
            P(None, "hist"),
            P("turn", None, "hist"),
            P("turn", "hist"),
            P("turn", "hist", None),
            P("turn"),
            P("turn", None),
            P(),
            P(),
        ),
        out_specs=(P("turn", None), P()),
        check_vma=False,
    )
```

```python
import functools

import jax
import jax.numpy as jnp
import numpy as np
from jax import lax
from jax.experimental import pallas as pl
from jax.experimental.pallas import tpu as pltpu
from jax.sharding import PartitionSpec as P

HANDS = 1326
LOW = 150
BASE = 245
SLOTS = HANDS - BASE
TILES = 9
WIDE = TILES * 128
ROWS = 17
ORDER = (2, 6, 3, 5, 0, 4, 1, 7)
EARLY = 5
CHUNK = 256
VMEM_LIMIT = 56 * 1024 * 1024
SMALL_LIMIT = 24 * 1024 * 1024


def slot_cards():
    first, second = np.triu_indices(52, 1)
    a = np.full((WIDE,), 200, np.int32)
    b = np.full((WIDE,), 201, np.int32)
    a[:SLOTS], b[:SLOTS] = first[BASE:], second[BASE:]
    return a, b


def compat_table():
    a, b = slot_cards()
    real = np.arange(WIDE) < SLOTS
    shares = (
        (a[:, None] == a[None, :])
        | (a[:, None] == b[None, :])
        | (b[:, None] == a[None, :])
        | (b[:, None] == b[None, :])
    )
    return (~shares & real[:, None] & real[None, :]).astype(np.float32)


def renamed(t, r):
    return jnp.where(r == 3, 4, 3), jnp.where(t == 4, 3, 4)


def source_lanes(a, b, t, r):
    card_t, card_r = renamed(t, r)
    off_t = jnp.where(card_t == 3, -4, 43)
    off_r = jnp.where(card_r == 3, -4, 43)
    has_t = (a == t) | (b == t)
    has_r = (a == r) | (b == r)
    from_t = jnp.where(a == t, b, a) + off_t
    from_r = jnp.where(a == r, b, a) + off_r
    one = jnp.where(has_t, from_t, jnp.where(has_r, from_r, -1))
    return jnp.where(has_t & has_r, 0, one)


def home_slots(lane, t, r):
    card_t, card_r = renamed(t, r)
    t_high, r_high = t >= 5, r >= 5
    none = jnp.int32(-1)
    name3 = jnp.where(t_high & (card_t == 3), t, jnp.where(r_high & (card_r == 3), r, none))
    name4 = jnp.where(t_high & (card_t == 4), t, jnp.where(r_high & (card_r == 4), r, none))
    of3 = lane < 48
    x = jnp.where(of3, lane + 4, lane - 43)
    p = jnp.where(of3, name3, name4)
    q = jnp.where(x == 4, name4, x)
    good = (lane < 95) & (p >= 5) & (q >= 5) & (x != t) & (x != r)
    low, high = jnp.minimum(p, q), jnp.maximum(p, q)
    u = low - 5
    slot = u * 46 - ((u * (u - 1)) >> 1) + high - low - 1
    return jnp.where(good, slot, -1)


def lanes_of(shape):
    return lax.broadcasted_iota(jnp.int32, shape, 1)


def pick(values, index):
    return jnp.take_along_axis(values, index, axis=1, mode="promise_in_bounds")


def tile(ref, j):
    return ref[:, 128 * j : 128 * j + 128]


def cards_of(table, j):
    return [jnp.broadcast_to(table[i : i + 1, 128 * j : 128 * j + 128], (8, 128)) for i in range(2)]


def pack_kernel(shifts, turn_card, river_card, policy_hbm, flop_reach, turn_policy, table, *rest):
    policy, staged, raw, own, low, in_sem, out_sem = rest[-7:]
    outs = rest[-7 - len(shifts) : -7]
    fetch = pltpu.make_async_copy(policy_hbm, policy, in_sem)
    fetch.start()
    me, t = lax.axis_index("hist"), turn_card[0]
    lane = lanes_of((8, 128))
    reach = flop_reach[...] * (turn_policy[...].astype(jnp.float32) * (1.0 / 256.0)) * (1.0 / 256.0)
    reach = jnp.concatenate([reach, jnp.zeros((16, 1408 - HANDS), jnp.float32)], axis=1)
    for j in range(11):
        raw[16 * j : 16 * j + 16, :] = reach[:, 128 * j : 128 * j + 128]
    wide = lanes_of((8, 1408))
    for p in range(2):
        reach = jnp.concatenate([raw[pl.ds(16 * j + p, 8, stride=2), :] for j in range(11)], axis=1)
        moved = pltpu.roll(reach, 1408 - BASE, 1)
        own[p] = jnp.where(wide < SLOTS, moved, 0.0)[:, :WIDE]
        moved = pltpu.roll(reach, 1408 - LOW, 1)
        low[p] = jnp.where(wide < 95, moved, 0.0)[:, :128]

    def one_river(out, rl, river):
        r = river_card[0, river]
        index = [source_lanes(*cards_of(table, j), t, r) for j in range(TILES)]
        tails = []
        for p in range(2):

            def aligned(start, count):
                row, shift = start >> 7, start & 127
                turn = (128 - shift) & 127
                rolled = [
                    pltpu.roll(policy[pl.ds(jnp.minimum(row + i, 662), 8, stride=663), :], turn, 1)
                    for i in range(count + 1)
                ]
                keep = lane < 128 - shift
                return [
                    jnp.where(keep, rolled[i], rolled[i + 1]).astype(jnp.float32) for i in range(count)
                ]

            start = p * 42432 + river * HANDS + LOW
            source = aligned(start, 1)[0] * low[p]
            plain = aligned(start + (BASE - LOW), TILES)
            for j in range(TILES):
                kept = plain[j] * own[p, :, 128 * j : 128 * j + 128]
                taken = pick(source, jnp.maximum(index[j], 0))
                value = jnp.where(index[j] >= 0, taken, kept)
                if j < 8:
                    out[rl, 8 * p + j] = value
                else:
                    tails.append(value)
        out[rl, 16] = tails[0] + pltpu.roll(tails[1], 64, 1)

    fetch.wait()
    stores = [pltpu.make_async_copy(staged.at[i], out, out_sem.at[i]) for i, out in enumerate(outs)]

    @pl.loop(0, len(outs))
    def _(i):
        shift = jnp.int32(shifts[0])
        for k in range(1, len(shifts)):
            shift = jnp.where(i == k, shifts[k], shift)
        river = ((me + shift) & 7) * 4
        for rl in range(4):
            one_river(staged.at[i], rl, river + rl)
        for k, store in enumerate(stores):

            @pl.when(i == k)
            def _(store=store):
                store.start()

    for store in stores:
        store.wait()


def pack(shifts, turn_cards, river_cards, policy, flop_reach, turn_policy, table, after):
    count = len(shifts)
    smem = pl.BlockSpec(memory_space=pltpu.SMEM)
    vmem = pl.BlockSpec(memory_space=pltpu.VMEM)
    anywhere = pl.BlockSpec(memory_space=pl.ANY)
    message = (4, ROWS, 8, 128)
    return pl.pallas_call(
        functools.partial(pack_kernel, shifts),
        out_shape=[jax.ShapeDtypeStruct(message, jnp.float32)] * count,
        in_specs=[smem] * 2 + [anywhere] + [vmem] * 3 + [anywhere] * len(after),
        out_specs=[anywhere] * count,
        scratch_shapes=[
            pltpu.VMEM((5304, 128), jnp.int32),
            pltpu.VMEM((count,) + message, jnp.float32),
            pltpu.VMEM((176, 128), jnp.float32),
            pltpu.VMEM((2, 8, WIDE), jnp.float32),
            pltpu.VMEM((2, 8, 128), jnp.float32),
            pltpu.SemaphoreType.DMA,
            pltpu.SemaphoreType.DMA((count,)),
        ],
        compiler_params=pltpu.CompilerParams(vmem_limit_bytes=VMEM_LIMIT),
        cost_estimate=pl.CostEstimate(flops=3000000, bytes_accessed=4000000, transcendentals=0),
        name="pack",
    )(turn_cards, river_cards, policy, flop_reach, turn_policy, table, *after)


def payoff_kernel(turn_card, river_card, ranks, compat, table, out, rows, strip):
    rl = pl.program_id(0)
    t = turn_card[0]
    r = river_card[0, 4 * lax.axis_index("hist") + rl]
    raw = ranks[...]
    value = (128 + (raw & 127)).astype(jnp.float32)
    for bit in range(6):
        value = value * jnp.where(((raw >> (7 + bit)) & 1) == 1, float(2 ** (2**bit)), 1.0)
    rows[...] = jnp.zeros_like(rows)
    rows[0:4, :HANDS] = value
    row = jnp.broadcast_to(rows[pl.ds(rl, 1), :], (8, 1408))
    plain = pltpu.roll(row, 1408 - BASE, 1)
    source = pltpu.roll(row, 1408 - LOW, 1)[:, :128]
    for j in range(TILES):
        index = source_lanes(*cards_of(table, j), t, r)
        taken = pick(source, jnp.maximum(index, 0))
        strip[:, 128 * j : 128 * j + 128] = jnp.where(index >= 0, taken, plain[:, 128 * j : 128 * j + 128])
    across = [
        jnp.broadcast_to(strip[0:1, 128 * j : 128 * j + 128], (128, 128)).astype(jnp.bfloat16)
        for j in range(TILES)
    ]
    code = jnp.where(lax.broadcasted_iota(jnp.int32, (8, WIDE), 0) == 0, strip[...], 0.0).astype(jnp.bfloat16)
    column = lax.dot_general(
        code, jnp.ones((8, 128), jnp.bfloat16), (((0,), (0,)), ((), ())), preferred_element_type=jnp.float32
    ).astype(jnp.bfloat16)
    for i in range(TILES):
        down = column[128 * i : 128 * i + 128]
        for j in range(TILES):
            mask = compat[128 * i : 128 * i + 128, 128 * j : 128 * j + 128]
            out[0, 128 * i : 128 * i + 128, 128 * j : 128 * j + 128] = jnp.minimum(
                jnp.maximum(across[j] - down, -mask), mask
            )


def payoffs(turn_cards, river_cards, ranks, compat, table):
    smem = pl.BlockSpec(memory_space=pltpu.SMEM)
    vmem = pl.BlockSpec(memory_space=pltpu.VMEM)
    return pl.pallas_call(
        payoff_kernel,
        grid=(4,),
        out_shape=jax.ShapeDtypeStruct((4, WIDE, WIDE), jnp.bfloat16),
        in_specs=[smem] * 2 + [vmem] * 3,
        out_specs=pl.BlockSpec((1, WIDE, WIDE), lambda i: (i, 0, 0)),
        scratch_shapes=[pltpu.VMEM((8, 1408), jnp.float32), pltpu.VMEM((8, WIDE), jnp.float32)],
        compiler_params=pltpu.CompilerParams(vmem_limit_bytes=SMALL_LIMIT),
        cost_estimate=pl.CostEstimate(flops=4 * 4 * WIDE * WIDE, bytes_accessed=10 * WIDE * WIDE, transcendentals=0),
        name="payoff",
    )(turn_cards, river_cards, ranks, compat, table)


def split_block(block, row, high, fine):
    lane = lanes_of((8, 128))
    for j in range(TILES):
        if j < 8:
            pair = [block[j], block[8 + j]]
        else:
            tails = block[16]
            pair = [jnp.where(lane < 64, v, 0.0) for v in (tails, pltpu.roll(tails, 64, 1))]
        both = jnp.concatenate(pair, axis=0)
        upper = both.astype(jnp.bfloat16)
        high[row : row + 16, 128 * j : 128 * j + 128] = upper
        fine[row : row + 16, 128 * j : 128 * j + 128] = (both - upper.astype(jnp.float32)).astype(jnp.bfloat16)


def chosen_rows(select, high, fine):
    parts = [jnp.dot(select[...], part[...], preferred_element_type=jnp.float32) for part in (high, fine)]
    return jnp.concatenate([part.astype(jnp.bfloat16) for part in parts], axis=0)


def choose_kernel(select, *rest):
    blocks, (out, high, fine) = rest[:-3], rest[-3:]
    for i, block in enumerate(blocks):
        split_block(block.at[0], 16 * i, high, fine)
    out[0] = chosen_rows(select, high, fine)


def choose(select, blocks):
    vmem = pl.BlockSpec(memory_space=pltpu.VMEM)
    rows = 16 * len(blocks)
    return pl.pallas_call(
        choose_kernel,
        grid=(4,),
        out_shape=jax.ShapeDtypeStruct((4, 256, WIDE), jnp.bfloat16),
        in_specs=[vmem] + [pl.BlockSpec((1, ROWS, 8, 128), lambda i: (i, 0, 0, 0))] * len(blocks),
        out_specs=pl.BlockSpec((1, 256, WIDE), lambda i: (i, 0, 0)),
        scratch_shapes=[pltpu.VMEM((rows, WIDE), jnp.bfloat16)] * 2,
        compiler_params=pltpu.CompilerParams(vmem_limit_bytes=SMALL_LIMIT),
        cost_estimate=pl.CostEstimate(flops=4 * 512 * rows * WIDE, bytes_accessed=5000000, transcendentals=0),
        name="choose",
    )(select, *blocks)


def reply_kernel(turn_card, river_card, payoff, early, select, scale, table, *rest):
    blocks, (out, high, fine) = rest[:-3], rest[-3:]
    t = turn_card[0]
    me = lax.axis_index("hist")
    lane = lanes_of((8, 128))
    out[...] = jnp.zeros_like(out)

    @pl.loop(0, 4)
    def _(rl):
        r = river_card[0, 4 * me + rl]
        for i, block in enumerate(blocks):
            split_block(block.at[rl], 16 * i, high, fine)
        chosen = early[rl] + chosen_rows(select, high, fine)
        home = home_slots(lane, t, r)
        home_tile, home_lane = home >> 7, home & 127
        first = [jnp.zeros((8, 128), jnp.float32)] * 8
        for start in range(0, WIDE, CHUNK):
            value = jnp.dot(chosen, payoff[rl, :, start : start + CHUNK], preferred_element_type=jnp.float32)
            value = (value[:128] + value[128:]) * scale[...]
            reply = jnp.maximum(value[:64], value[64:])
            for j in range(start // 128, min(start + CHUNK, WIDE) // 128):
                moved = source_lanes(*cards_of(table, j), t, r) >= 0
                for g in range(8):
                    part = reply[8 * g : 8 * g + 8, 128 * j - start : 128 * j - start + 128]
                    out[g, 1 + j] += jnp.where(moved, 0.0, part)
                    first[g] = jnp.where(home_tile == j, pick(part, home_lane), first[g])
        for g in range(8):
            out[g, 0] += first[g]


def replies(turn_cards, river_cards, payoff, early, select, scale, table, blocks):
    smem = pl.BlockSpec(memory_space=pltpu.SMEM)
    vmem = pl.BlockSpec(memory_space=pltpu.VMEM)
    rows = 16 * len(blocks)
    return pl.pallas_call(
        reply_kernel,
        out_shape=jax.ShapeDtypeStruct((8, TILES + 1, 8, 128), jnp.float32),
        in_specs=[smem] * 2 + [vmem] * (5 + len(blocks)),
        out_specs=vmem,
        scratch_shapes=[pltpu.VMEM((rows, WIDE), jnp.bfloat16)] * 2,
        compiler_params=pltpu.CompilerParams(vmem_limit_bytes=SMALL_LIMIT),
        cost_estimate=pl.CostEstimate(
            flops=4 * 2 * 256 * WIDE * WIDE, bytes_accessed=8 * WIDE * WIDE, transcendentals=0
        ),
        name="reply",
    )(turn_cards, river_cards, payoff, early, select, scale, table, *blocks)


def flat(nodes):
    rows = jnp.transpose(nodes, (0, 2, 1, 3)).reshape(64, TILES + 1, 128)
    body = rows[:, 1:].reshape(64, WIDE)[:, :SLOTS]
    return jnp.concatenate([jnp.zeros((64, LOW), jnp.float32), rows[:, 0, :95], body], axis=1).reshape(-1)


def turn_sum(value, size):
    pairs = [(i, i ^ 1) for i in range(size)]
    half = value.shape[0] // 2
    core = lax.axis_index("turn") & 1
    keep = lax.dynamic_slice_in_dim(value, core * half, half, 0)
    give = lax.dynamic_slice_in_dim(value, (1 - core) * half, half, 0)
    total = keep + lax.ppermute(give, "turn", pairs)
    step = 2
    while step < size:
        for flip in (1, 3):
            total = total + lax.ppermute(total, "turn", [(i, i ^ (flip * step)) for i in range(size)])
        step *= 4
    return total, pairs, core


def per_device(flop_reach, turn_policy, river_policy, hand_rank, turn_cards, river_cards, children, pot):
    groups = lax.axis_size("hist")
    turns = lax.axis_size("turn")
    me = lax.axis_index("hist")
    table = jnp.asarray(np.stack(slot_cards()))
    compat = jnp.asarray(compat_table(), jnp.bfloat16)
    policy = river_policy.reshape(5304, 128)
    common = (turn_cards, river_cards, policy, jnp.transpose(flop_reach), jnp.transpose(turn_policy[0]), table)

    def send(block, s):
        return lax.ppermute(block, "hist", [(i, (i + s) % groups) for i in range(groups)])

    got = {}

    def exchange(shifts, after):
        for s, block in zip(shifts, pack(shifts, *common, after)):
            got[s] = send(block, s) if s else block
        return [got[s] for s in shifts]

    first = exchange((2, 6), [])
    exchange((3, 5), [])
    exchange((4, 1, 7, 0), first)
    payoff = payoffs(turn_cards, river_cards, hand_rank[0], compat, table)
    child = jnp.transpose(children).reshape(128)
    turn_of = jnp.zeros((8,), jnp.int32).at[jnp.array(ORDER)].set(jnp.arange(8, dtype=jnp.int32))
    place = (turn_of[(me - (child >> 4)) & 7] << 4) + ((child & 1) << 3) + ((child >> 1) & 7)
    select = (place[:, None] == jnp.arange(128)[None, :]).astype(jnp.bfloat16)
    scale = jnp.sum(
        jnp.where(child[:, None] == jnp.arange(128)[None, :], pot.astype(jnp.float32)[None, :], 0.0),
        axis=1,
        keepdims=True,
    )
    early = choose(select[:, : 16 * EARLY], [got[s] for s in ORDER[:EARLY]])
    late = [got[s] for s in ORDER[EARLY:]]
    partial = replies(turn_cards, river_cards, payoff, early, select[:, 16 * EARLY :], scale, table, late)
    arrived = lax.all_to_all(partial, "hist", 0, 0, tiled=True)
    value = jnp.sum(arrived, axis=0) * (1.0 / 32.0)
    half, pairs, core = turn_sum(value, turns)
    both = jnp.concatenate([value, half * (1.0 / turns)], axis=0)
    spread = lax.all_to_all(jnp.broadcast_to(both, (groups,) + both.shape), "hist", 0, 0, tiled=True)
    here = spread[:, TILES + 1 :]
    there = lax.ppermute(here, "turn", pairs)
    mean = jnp.concatenate([jnp.where(core == 0, here, there), jnp.where(core == 0, there, here)], axis=1)
    return (flat(spread[:, : TILES + 1]).reshape(1, -1), flat(mean))


def solution(mesh):
    return jax.shard_map(
        per_device,
        mesh=mesh,
        in_specs=(
            P(None, "hist"),
            P("turn", None, "hist"),
            P("turn", "hist"),
            P("turn", "hist", None),
            P("turn"),
            P("turn", None),
            P(),
            P(),
        ),
        out_specs=(P("turn", None), P()),
        check_vma=False,
    )
```

```python
import functools

import jax
import jax.numpy as jnp
import numpy as np
from jax import lax
from jax.experimental import pallas as pl
from jax.experimental.pallas import tpu as pltpu
from jax.sharding import PartitionSpec as P

HANDS = 1326
LOW = 150
BASE = 245
SLOTS = HANDS - BASE
TILES = 9
WIDE = TILES * 128
ROWS = 17
ORDER = (2, 6, 3, 5, 0, 4, 1, 7)
EARLY = 5
CHUNK = 256
FETCH = 56
VMEM_LIMIT = 56 * 1024 * 1024
SMALL_LIMIT = 16 * 1024 * 1024


def slot_cards():
    first, second = np.triu_indices(52, 1)
    a = np.full((WIDE,), 200, np.int32)
    b = np.full((WIDE,), 201, np.int32)
    a[:SLOTS], b[:SLOTS] = first[BASE:], second[BASE:]
    return a, b


def compat_table():
    a, b = slot_cards()
    real = np.arange(WIDE) < SLOTS
    shares = (
        (a[:, None] == a[None, :])
        | (a[:, None] == b[None, :])
        | (b[:, None] == a[None, :])
        | (b[:, None] == b[None, :])
    )
    return (~shares & real[:, None] & real[None, :]).astype(np.float32)


def renamed(t, r):
    return jnp.where(r == 3, 4, 3), jnp.where(t == 4, 3, 4)


def source_lanes(a, b, t, r):
    card_t, card_r = renamed(t, r)
    off_t = jnp.where(card_t == 3, -4, 43)
    off_r = jnp.where(card_r == 3, -4, 43)
    has_t = (a == t) | (b == t)
    has_r = (a == r) | (b == r)
    from_t = jnp.where(a == t, b, a) + off_t
    from_r = jnp.where(a == r, b, a) + off_r
    one = jnp.where(has_t, from_t, jnp.where(has_r, from_r, -1))
    return jnp.where(has_t & has_r, 0, one)


def home_slots(lane, t, r):
    card_t, card_r = renamed(t, r)
    t_high, r_high = t >= 5, r >= 5
    none = jnp.int32(-1)
    name3 = jnp.where(t_high & (card_t == 3), t, jnp.where(r_high & (card_r == 3), r, none))
    name4 = jnp.where(t_high & (card_t == 4), t, jnp.where(r_high & (card_r == 4), r, none))
    of3 = lane < 48
    x = jnp.where(of3, lane + 4, lane - 43)
    p = jnp.where(of3, name3, name4)
    q = jnp.where(x == 4, name4, x)
    good = (lane < 95) & (p >= 5) & (q >= 5) & (x != t) & (x != r)
    low, high = jnp.minimum(p, q), jnp.maximum(p, q)
    u = low - 5
    slot = u * 46 - ((u * (u - 1)) >> 1) + high - low - 1
    return jnp.where(good, slot, -1)


def lanes_of(shape):
    return lax.broadcasted_iota(jnp.int32, shape, 1)


def pick(values, index):
    return jnp.take_along_axis(values, index, axis=1, mode="promise_in_bounds")


def tile(ref, j):
    return ref[:, 128 * j : 128 * j + 128]


def cards_of(table, j):
    return [jnp.broadcast_to(table[i : i + 1, 128 * j : 128 * j + 128], (8, 128)) for i in range(2)]


def first_row(group, p):
    return (p * 42432 + group * 4 * HANDS + LOW) >> 7


def pack_kernel(shifts, turn_card_hbm, river_card_hbm, policy_hbm, flop_hbm, turn_hbm, table_hbm, *rest):
    turn_card, river_card, flop_reach, turn_policy, table, policy, raw, own, low, in_sem, row_sem = rest[-11:]
    outs = rest[-11 - len(shifts) : -11]
    small = [
        pltpu.make_async_copy(source, to, in_sem.at[i])
        for i, (source, to) in enumerate(
            zip(
                (turn_card_hbm, river_card_hbm, flop_hbm, turn_hbm, table_hbm),
                (turn_card, river_card, flop_reach, turn_policy, table),
            )
        )
    ]
    for fetch in small:
        fetch.start()
    fetches = []
    for i, shift in enumerate(shifts):
        for p in range(2):
            base = first_row((lax.axis_index("hist") + shift) & 7, p)
            for g in range(8):
                wanted = ((663 * g + base) >> 3) << 3
                start = jnp.minimum(wanted, 5304 - FETCH)
                place = 16 + 72 * g - jnp.where(g > (base & 7), 8, 0) - (wanted - start)
                fetches.append(
                    pltpu.make_async_copy(
                        policy_hbm.at[pl.ds(pl.multiple_of(start, 8), FETCH)],
                        policy.at[i, p, pl.ds(pl.multiple_of(place, 8), FETCH)],
                        row_sem.at[i, p, g],
                    )
                )
                fetches[-1].start()
    for fetch in small:
        fetch.wait()
    me, t = lax.axis_index("hist"), turn_card[0]
    lane = lanes_of((8, 128))
    reach = flop_reach[...] * (turn_policy[...].astype(jnp.float32) * (1.0 / 256.0)) * (1.0 / 256.0)
    reach = jnp.concatenate([reach, jnp.zeros((16, 1408 - HANDS), jnp.float32)], axis=1)
    for j in range(11):
        raw[16 * j : 16 * j + 16, :] = reach[:, 128 * j : 128 * j + 128]
    wide = lanes_of((8, 1408))
    for p in range(2):
        reach = jnp.concatenate([raw[pl.ds(16 * j + p, 8, stride=2), :] for j in range(11)], axis=1)
        moved = pltpu.roll(reach, 1408 - BASE, 1)
        own[p] = jnp.where(wide < SLOTS, moved, 0.0)[:, :WIDE]
        moved = pltpu.roll(reach, 1408 - LOW, 1)
        low[p] = jnp.where(wide < 95, moved, 0.0)[:, :128]

    def one_river(out, i, group, rl):
        river = 4 * group + rl
        r = river_card[0, river]
        index = [source_lanes(*cards_of(table, j), t, r) for j in range(TILES)]
        tails = []
        for p in range(2):

            base = first_row(group, p)

            def aligned(start, count, p=p, base=base):
                row, shift = start >> 7, start & 127
                turn = (128 - shift) & 127
                rolled = [
                    pltpu.roll(policy[i, p, pl.ds(jnp.minimum(row + k, 662) - base + (base & 7) + 16, 8, stride=71), :], turn, 1)
                    for k in range(count + 1)
                ]
                keep = lane < 128 - shift
                return [
                    jnp.where(keep, rolled[k], rolled[k + 1]).astype(jnp.float32) for k in range(count)
                ]

            start = p * 42432 + river * HANDS + LOW
            source = aligned(start, 1)[0] * low[p]
            plain = aligned(start + (BASE - LOW), TILES)
            for j in range(TILES):
                kept = plain[j] * own[p, :, 128 * j : 128 * j + 128]
                taken = pick(source, jnp.maximum(index[j], 0))
                value = jnp.where(index[j] >= 0, taken, kept)
                if j < 8:
                    out[rl, 8 * p + j] = value
                else:
                    tails.append(value)
        out[rl, 16] = tails[0] + pltpu.roll(tails[1], 64, 1)

    for fetch in fetches:
        fetch.wait()
    for i, (shift, out) in enumerate(zip(shifts, outs)):

        @pl.loop(0, 2)
        def _(pair, i=i, out=out, group=(me + shift) & 7):
            one_river(out, i, group, 2 * pair)
            one_river(out, i, group, 2 * pair + 1)


def pack(shifts, turn_cards, river_cards, policy, flop_reach, turn_policy, table, after):
    anywhere = pl.BlockSpec(memory_space=pl.ANY)
    count = len(shifts)
    return pl.pallas_call(
        functools.partial(pack_kernel, shifts),
        out_shape=[jax.ShapeDtypeStruct((4, ROWS, 8, 128), jnp.float32)] * count,
        in_specs=[anywhere] * (6 + len(after)),
        out_specs=[pl.BlockSpec(memory_space=pltpu.VMEM)] * count,
        scratch_shapes=[
            pltpu.SMEM((1,), jnp.int32),
            pltpu.SMEM((1, 32), jnp.int32),
            pltpu.VMEM((16, HANDS), jnp.float32),
            pltpu.VMEM((16, HANDS), jnp.int32),
            pltpu.VMEM((2, WIDE), jnp.int32),
            pltpu.VMEM((count, 2, 584, 128), jnp.int32),
            pltpu.VMEM((176, 128), jnp.float32),
            pltpu.VMEM((2, 8, WIDE), jnp.float32),
            pltpu.VMEM((2, 8, 128), jnp.float32),
            pltpu.SemaphoreType.DMA((5,)),
            pltpu.SemaphoreType.DMA((count, 2, 8)),
        ],
        compiler_params=pltpu.CompilerParams(vmem_limit_bytes=VMEM_LIMIT),
        cost_estimate=pl.CostEstimate(flops=3000000, bytes_accessed=4000000, transcendentals=0),
        name="pack",
    )(turn_cards, river_cards, policy, flop_reach, turn_policy, table, *after)


def payoff_kernel(turn_card, river_card, ranks, compat, table, out, rows, strip):
    rl = pl.program_id(0)
    t = turn_card[0]
    r = river_card[0, 4 * lax.axis_index("hist") + rl]
    raw = ranks[...]
    value = (128 + (raw & 127)).astype(jnp.float32)
    for bit in range(6):
        value = value * jnp.where(((raw >> (7 + bit)) & 1) == 1, float(2 ** (2**bit)), 1.0)
    rows[...] = jnp.zeros_like(rows)
    rows[0:4, :HANDS] = value
    row = jnp.broadcast_to(rows[pl.ds(rl, 1), :], (8, 1408))
    plain = pltpu.roll(row, 1408 - BASE, 1)
    source = pltpu.roll(row, 1408 - LOW, 1)[:, :128]
    for j in range(TILES):
        index = source_lanes(*cards_of(table, j), t, r)
        taken = pick(source, jnp.maximum(index, 0))
        strip[:, 128 * j : 128 * j + 128] = jnp.where(index >= 0, taken, plain[:, 128 * j : 128 * j + 128])
    across = [
        jnp.broadcast_to(strip[0:1, 128 * j : 128 * j + 128], (128, 128)).astype(jnp.bfloat16)
        for j in range(TILES)
    ]
    code = jnp.where(lax.broadcasted_iota(jnp.int32, (8, WIDE), 0) == 0, strip[...], 0.0).astype(jnp.bfloat16)
    column = lax.dot_general(
        code, jnp.ones((8, 128), jnp.bfloat16), (((0,), (0,)), ((), ())), preferred_element_type=jnp.float32
    ).astype(jnp.bfloat16)
    for i in range(TILES):
        down = column[128 * i : 128 * i + 128]
        for j in range(TILES):
            mask = compat[128 * i : 128 * i + 128, 128 * j : 128 * j + 128]
            out[0, 128 * i : 128 * i + 128, 128 * j : 128 * j + 128] = jnp.minimum(
                jnp.maximum(across[j] - down, -mask), mask
            )


def payoffs(turn_cards, river_cards, ranks, compat, table):
    smem = pl.BlockSpec(memory_space=pltpu.SMEM)
    vmem = pl.BlockSpec(memory_space=pltpu.VMEM)
    return pl.pallas_call(
        payoff_kernel,
        grid=(4,),
        out_shape=jax.ShapeDtypeStruct((4, WIDE, WIDE), jnp.bfloat16),
        in_specs=[smem] * 2 + [vmem] * 3,
        out_specs=pl.BlockSpec((1, WIDE, WIDE), lambda i: (i, 0, 0)),
        scratch_shapes=[pltpu.VMEM((8, 1408), jnp.float32), pltpu.VMEM((8, WIDE), jnp.float32)],
        compiler_params=pltpu.CompilerParams(vmem_limit_bytes=SMALL_LIMIT),
        cost_estimate=pl.CostEstimate(flops=4 * 4 * WIDE * WIDE, bytes_accessed=10 * WIDE * WIDE, transcendentals=0),
        name="payoff",
    )(turn_cards, river_cards, ranks, compat, table)


def split_block(block, row, high, fine):
    lane = lanes_of((8, 128))
    for j in range(TILES):
        if j < 8:
            pair = [block[j], block[8 + j]]
        else:
            tails = block[16]
            pair = [jnp.where(lane < 64, v, 0.0) for v in (tails, pltpu.roll(tails, 64, 1))]
        both = jnp.concatenate(pair, axis=0)
        upper = both.astype(jnp.bfloat16)
        high[row : row + 16, 128 * j : 128 * j + 128] = upper
        fine[row : row + 16, 128 * j : 128 * j + 128] = (both - upper.astype(jnp.float32)).astype(jnp.bfloat16)


def chosen_rows(select, high, fine):
    parts = [jnp.dot(select[...], part[...], preferred_element_type=jnp.float32) for part in (high, fine)]
    return jnp.concatenate([part.astype(jnp.bfloat16) for part in parts], axis=0)


def choose_kernel(select, *rest):
    blocks, (out, high, fine) = rest[:-3], rest[-3:]
    for i, block in enumerate(blocks):
        split_block(block.at[0], 16 * i, high, fine)
    out[0] = chosen_rows(select, high, fine)


def choose(select, blocks):
    vmem = pl.BlockSpec(memory_space=pltpu.VMEM)
    rows = 16 * len(blocks)
    return pl.pallas_call(
        choose_kernel,
        grid=(4,),
        out_shape=jax.ShapeDtypeStruct((4, 256, WIDE), jnp.bfloat16),
        in_specs=[vmem] + [pl.BlockSpec((1, ROWS, 8, 128), lambda i: (i, 0, 0, 0))] * len(blocks),
        out_specs=pl.BlockSpec((1, 256, WIDE), lambda i: (i, 0, 0)),
        scratch_shapes=[pltpu.VMEM((rows, WIDE), jnp.bfloat16)] * 2,
        compiler_params=pltpu.CompilerParams(vmem_limit_bytes=SMALL_LIMIT),
        cost_estimate=pl.CostEstimate(flops=4 * 512 * rows * WIDE, bytes_accessed=5000000, transcendentals=0),
        name="choose",
    )(select, *blocks)


def reply_kernel(turn_card, river_card, payoff, early, select, scale, table, *rest):
    blocks, (out, high, fine) = rest[:-3], rest[-3:]
    t = turn_card[0]
    me = lax.axis_index("hist")
    lane = lanes_of((8, 128))
    rl = pl.program_id(0)

    @pl.when(rl == 0)
    def _():
        out[...] = jnp.zeros_like(out)

    r = river_card[0, 4 * me + rl]
    for i, block in enumerate(blocks):
        split_block(block.at[0], 16 * i, high, fine)
    chosen = early[rl] + chosen_rows(select, high, fine)
    home = home_slots(lane, t, r)
    home_tile, home_lane = home >> 7, home & 127
    first = [jnp.zeros((8, 128), jnp.float32)] * 8
    for start in range(0, WIDE, CHUNK):
        value = jnp.dot(chosen, payoff[rl, :, start : start + CHUNK], preferred_element_type=jnp.float32)
        value = (value[:128] + value[128:]) * scale[...]
        reply = jnp.maximum(value[:64], value[64:])
        for j in range(start // 128, min(start + CHUNK, WIDE) // 128):
            moved = source_lanes(*cards_of(table, j), t, r) >= 0
            for g in range(8):
                part = reply[8 * g : 8 * g + 8, 128 * j - start : 128 * j - start + 128]
                out[g, 1 + j] += jnp.where(moved, 0.0, part)
                first[g] = jnp.where(home_tile == j, pick(part, home_lane), first[g])
    for g in range(8):
        out[g, 0] += first[g]


def replies(turn_cards, river_cards, payoff, early, select, scale, table, blocks):
    smem = pl.BlockSpec(memory_space=pltpu.SMEM)
    vmem = pl.BlockSpec(memory_space=pltpu.VMEM)
    rows = 16 * len(blocks)
    return pl.pallas_call(
        reply_kernel,
        grid=(4,),
        out_shape=jax.ShapeDtypeStruct((8, TILES + 1, 8, 128), jnp.float32),
        in_specs=[smem] * 2
        + [vmem] * 5
        + [pl.BlockSpec((1, ROWS, 8, 128), lambda i: (i, 0, 0, 0))] * len(blocks),
        out_specs=vmem,
        scratch_shapes=[pltpu.VMEM((rows, WIDE), jnp.bfloat16)] * 2,
        compiler_params=pltpu.CompilerParams(vmem_limit_bytes=SMALL_LIMIT),
        cost_estimate=pl.CostEstimate(
            flops=4 * 2 * 256 * WIDE * WIDE, bytes_accessed=8 * WIDE * WIDE, transcendentals=0
        ),
        name="reply",
    )(turn_cards, river_cards, payoff, early, select, scale, table, *blocks)


def flat(nodes):
    rows = jnp.transpose(nodes, (0, 2, 1, 3)).reshape(64, TILES + 1, 128)
    body = rows[:, 1:].reshape(64, WIDE)[:, :SLOTS]
    return jnp.concatenate([jnp.zeros((64, LOW), jnp.float32), rows[:, 0, :95], body], axis=1).reshape(-1)


def turn_sum(value, size):
    pairs = [(i, i ^ 1) for i in range(size)]
    half = value.shape[0] // 2
    core = lax.axis_index("turn") & 1
    keep = lax.dynamic_slice_in_dim(value, core * half, half, 0)
    give = lax.dynamic_slice_in_dim(value, (1 - core) * half, half, 0)
    total = keep + lax.ppermute(give, "turn", pairs)
    step = 2
    while step < size:
        for flip in (1, 3):
            total = total + lax.ppermute(total, "turn", [(i, i ^ (flip * step)) for i in range(size)])
        step *= 4
    return total, pairs, core


def per_device(flop_reach, turn_policy, river_policy, hand_rank, turn_cards, river_cards, children, pot):
    groups = lax.axis_size("hist")
    turns = lax.axis_size("turn")
    me = lax.axis_index("hist")
    table = jnp.asarray(np.stack(slot_cards()))
    compat = jnp.asarray(compat_table(), jnp.bfloat16)
    policy = river_policy.reshape(5304, 128)
    common = (turn_cards, river_cards, policy, jnp.transpose(flop_reach), jnp.transpose(turn_policy[0]), table)

    def send(block, s):
        return lax.ppermute(block, "hist", [(i, (i + s) % groups) for i in range(groups)])

    got = {}

    def exchange(shifts, after):
        for s, block in zip(shifts, pack(shifts, *common, after)):
            got[s] = send(block, s) if s else block
        return [got[s] for s in shifts]

    first = exchange((2, 6), [])
    exchange((3, 5), [])
    exchange((4, 1, 7, 0), [])
    payoff = payoffs(turn_cards, river_cards, hand_rank[0], compat, table)
    child = jnp.transpose(children).reshape(128)
    turn_of = jnp.zeros((8,), jnp.int32).at[jnp.array(ORDER)].set(jnp.arange(8, dtype=jnp.int32))
    place = (turn_of[(me - (child >> 4)) & 7] << 4) + ((child & 1) << 3) + ((child >> 1) & 7)
    select = (place[:, None] == jnp.arange(128)[None, :]).astype(jnp.bfloat16)
    scale = jnp.sum(
        jnp.where(child[:, None] == jnp.arange(128)[None, :], pot.astype(jnp.float32)[None, :], 0.0),
        axis=1,
        keepdims=True,
    )
    early = choose(select[:, : 16 * EARLY], [got[s] for s in ORDER[:EARLY]])
    late = [got[s] for s in ORDER[EARLY:]]
    partial = replies(turn_cards, river_cards, payoff, early, select[:, 16 * EARLY :], scale, table, late)
    arrived = lax.all_to_all(partial, "hist", 0, 0, tiled=True)
    value = jnp.sum(arrived, axis=0) * (1.0 / 32.0)
    half, pairs, core = turn_sum(value, turns)
    both = jnp.concatenate([value, half * (1.0 / turns)], axis=0)
    spread = lax.all_to_all(jnp.broadcast_to(both, (groups,) + both.shape), "hist", 0, 0, tiled=True)
    here = spread[:, TILES + 1 :]
    there = lax.ppermute(here, "turn", pairs)
    mean = jnp.concatenate([jnp.where(core == 0, here, there), jnp.where(core == 0, there, here)], axis=1)
    return (flat(spread[:, : TILES + 1]).reshape(1, -1), flat(mean))


def solution(mesh):
    return jax.shard_map(
        per_device,
        mesh=mesh,
        in_specs=(
            P(None, "hist"),
            P("turn", None, "hist"),
            P("turn", "hist"),
            P("turn", "hist", None),
            P("turn"),
            P("turn", None),
            P(),
            P(),
        ),
        out_specs=(P("turn", None), P()),
        check_vma=False,
    )
```

```python
import functools

import jax
import jax.numpy as jnp
import numpy as np
from jax import lax
from jax.experimental import pallas as pl
from jax.experimental.pallas import tpu as pltpu
from jax.sharding import PartitionSpec as P

HANDS = 1326
LOW = 150
BASE = 245
SLOTS = HANDS - BASE
TILES = 9
WIDE = TILES * 128
ROWS = 17
ORDER = (2, 6, 3, 5, 0, 4, 1, 7)
EARLY = 5
CHUNK = 1152
FETCH = 56
VMEM_LIMIT = 56 * 1024 * 1024
SMALL_LIMIT = 24 * 1024 * 1024


def slot_cards():
    first, second = np.triu_indices(52, 1)
    a = np.full((WIDE,), 200, np.int32)
    b = np.full((WIDE,), 201, np.int32)
    a[:SLOTS], b[:SLOTS] = first[BASE:], second[BASE:]
    return a, b


def compat_table():
    a, b = slot_cards()
    real = np.arange(WIDE) < SLOTS
    shares = (
        (a[:, None] == a[None, :])
        | (a[:, None] == b[None, :])
        | (b[:, None] == a[None, :])
        | (b[:, None] == b[None, :])
    )
    return (~shares & real[:, None] & real[None, :]).astype(np.float32)


def renamed(t, r):
    return jnp.where(r == 3, 4, 3), jnp.where(t == 4, 3, 4)


def source_lanes(a, b, t, r):
    card_t, card_r = renamed(t, r)
    off_t = jnp.where(card_t == 3, -4, 43)
    off_r = jnp.where(card_r == 3, -4, 43)
    has_t = (a == t) | (b == t)
    has_r = (a == r) | (b == r)
    from_t = jnp.where(a == t, b, a) + off_t
    from_r = jnp.where(a == r, b, a) + off_r
    one = jnp.where(has_t, from_t, jnp.where(has_r, from_r, -1))
    return jnp.where(has_t & has_r, 0, one)


def home_slots(lane, t, r):
    card_t, card_r = renamed(t, r)
    t_high, r_high = t >= 5, r >= 5
    none = jnp.int32(-1)
    name3 = jnp.where(t_high & (card_t == 3), t, jnp.where(r_high & (card_r == 3), r, none))
    name4 = jnp.where(t_high & (card_t == 4), t, jnp.where(r_high & (card_r == 4), r, none))
    of3 = lane < 48
    x = jnp.where(of3, lane + 4, lane - 43)
    p = jnp.where(of3, name3, name4)
    q = jnp.where(x == 4, name4, x)
    good = (lane < 95) & (p >= 5) & (q >= 5) & (x != t) & (x != r)
    low, high = jnp.minimum(p, q), jnp.maximum(p, q)
    u = low - 5
    slot = u * 46 - ((u * (u - 1)) >> 1) + high - low - 1
    return jnp.where(good, slot, -1)


def lanes_of(shape):
    return lax.broadcasted_iota(jnp.int32, shape, 1)


def pick(values, index):
    return jnp.take_along_axis(values, index, axis=1, mode="promise_in_bounds")


def tile(ref, j):
    return ref[:, 128 * j : 128 * j + 128]


def cards_of(table, j):
    return [jnp.broadcast_to(table[i : i + 1, 128 * j : 128 * j + 128], (8, 128)) for i in range(2)]


def first_row(group, p):
    return (p * 42432 + group * 4 * HANDS + LOW) >> 7


def pack_kernel(shifts, turn_card_hbm, river_card_hbm, policy_hbm, flop_hbm, turn_hbm, table_hbm, *rest):
    turn_card, river_card, flop_reach, turn_policy, table, policy, raw, own, low, in_sem, row_sem = rest[-11:]
    outs = rest[-11 - len(shifts) : -11]
    small = [
        pltpu.make_async_copy(source, to, in_sem.at[i])
        for i, (source, to) in enumerate(
            zip(
                (turn_card_hbm, river_card_hbm, flop_hbm, turn_hbm, table_hbm),
                (turn_card, river_card, flop_reach, turn_policy, table),
            )
        )
    ]
    for fetch in small:
        fetch.start()
    fetches = []
    for i, shift in enumerate(shifts):
        for p in range(2):
            base = first_row((lax.axis_index("hist") + shift) & 7, p)
            for g in range(8):
                wanted = ((663 * g + base) >> 3) << 3
                start = jnp.minimum(wanted, 5304 - FETCH)
                place = 16 + 72 * g - jnp.where(g > (base & 7), 8, 0) - (wanted - start)
                fetches.append(
                    pltpu.make_async_copy(
                        policy_hbm.at[pl.ds(pl.multiple_of(start, 8), FETCH)],
                        policy.at[i, p, pl.ds(pl.multiple_of(place, 8), FETCH)],
                        row_sem.at[i, p, g],
                    )
                )
                fetches[-1].start()
    for fetch in small:
        fetch.wait()
    me, t = lax.axis_index("hist"), turn_card[0]
    lane = lanes_of((8, 128))
    reach = flop_reach[...] * (turn_policy[...].astype(jnp.float32) * (1.0 / 256.0)) * (1.0 / 256.0)
    reach = jnp.concatenate([reach, jnp.zeros((16, 1408 - HANDS), jnp.float32)], axis=1)
    for j in range(11):
        raw[16 * j : 16 * j + 16, :] = reach[:, 128 * j : 128 * j + 128]
    wide = lanes_of((8, 1408))
    for p in range(2):
        reach = jnp.concatenate([raw[pl.ds(16 * j + p, 8, stride=2), :] for j in range(11)], axis=1)
        moved = pltpu.roll(reach, 1408 - BASE, 1)
        own[p] = jnp.where(wide < SLOTS, moved, 0.0)[:, :WIDE]
        moved = pltpu.roll(reach, 1408 - LOW, 1)
        low[p] = jnp.where(wide < 95, moved, 0.0)[:, :128]

    def one_river(out, i, group, rl):
        river = 4 * group + rl
        r = river_card[0, river]
        index = [source_lanes(*cards_of(table, j), t, r) for j in range(TILES)]
        tails = []
        for p in range(2):

            base = first_row(group, p)

            def aligned(start, count, p=p, base=base):
                row, shift = start >> 7, start & 127
                turn = (128 - shift) & 127
                rolled = [
                    pltpu.roll(policy[i, p, pl.ds(jnp.minimum(row + k, 662) - base + (base & 7) + 16, 8, stride=71), :], turn, 1)
                    for k in range(count + 1)
                ]
                keep = lane < 128 - shift
                return [
                    jnp.where(keep, rolled[k], rolled[k + 1]).astype(jnp.float32) for k in range(count)
                ]

            start = p * 42432 + river * HANDS + LOW
            source = aligned(start, 1)[0] * low[p]
            plain = aligned(start + (BASE - LOW), TILES)
            for j in range(TILES):
                kept = plain[j] * own[p, :, 128 * j : 128 * j + 128]
                taken = pick(source, jnp.maximum(index[j], 0))
                value = jnp.where(index[j] >= 0, taken, kept)
                if j < 8:
                    out[rl, 8 * p + j] = value
                else:
                    tails.append(value)
        out[rl, 16] = tails[0] + pltpu.roll(tails[1], 64, 1)

    for fetch in fetches:
        fetch.wait()
    for i, (shift, out) in enumerate(zip(shifts, outs)):

        @pl.loop(0, 2)
        def _(pair, i=i, out=out, group=(me + shift) & 7):
            one_river(out, i, group, 2 * pair)
            one_river(out, i, group, 2 * pair + 1)


def pack(shifts, turn_cards, river_cards, policy, flop_reach, turn_policy, table, after):
    anywhere = pl.BlockSpec(memory_space=pl.ANY)
    count = len(shifts)
    return pl.pallas_call(
        functools.partial(pack_kernel, shifts),
        out_shape=[jax.ShapeDtypeStruct((4, ROWS, 8, 128), jnp.float32)] * count,
        in_specs=[anywhere] * (6 + len(after)),
        out_specs=[pl.BlockSpec(memory_space=pltpu.VMEM)] * count,
        scratch_shapes=[
            pltpu.SMEM((1,), jnp.int32),
            pltpu.SMEM((1, 32), jnp.int32),
            pltpu.VMEM((16, HANDS), jnp.float32),
            pltpu.VMEM((16, HANDS), jnp.int32),
            pltpu.VMEM((2, WIDE), jnp.int32),
            pltpu.VMEM((count, 2, 584, 128), jnp.int32),
            pltpu.VMEM((176, 128), jnp.float32),
            pltpu.VMEM((2, 8, WIDE), jnp.float32),
            pltpu.VMEM((2, 8, 128), jnp.float32),
            pltpu.SemaphoreType.DMA((5,)),
            pltpu.SemaphoreType.DMA((count, 2, 8)),
        ],
        compiler_params=pltpu.CompilerParams(vmem_limit_bytes=VMEM_LIMIT),
        cost_estimate=pl.CostEstimate(flops=3000000, bytes_accessed=4000000, transcendentals=0),
        name="pack",
    )(turn_cards, river_cards, policy, flop_reach, turn_policy, table, *after)


def payoff_kernel(turn_card, river_card, ranks, compat, table, out, rows, strip):
    rl = pl.program_id(0)
    t = turn_card[0]
    r = river_card[0, 4 * lax.axis_index("hist") + rl]
    raw = ranks[...]
    value = (128 + (raw & 127)).astype(jnp.float32)
    for bit in range(6):
        value = value * jnp.where(((raw >> (7 + bit)) & 1) == 1, float(2 ** (2**bit)), 1.0)
    rows[...] = jnp.zeros_like(rows)
    rows[0:4, :HANDS] = value
    row = jnp.broadcast_to(rows[pl.ds(rl, 1), :], (8, 1408))
    plain = pltpu.roll(row, 1408 - BASE, 1)
    source = pltpu.roll(row, 1408 - LOW, 1)[:, :128]
    for j in range(TILES):
        index = source_lanes(*cards_of(table, j), t, r)
        taken = pick(source, jnp.maximum(index, 0))
        strip[:, 128 * j : 128 * j + 128] = jnp.where(index >= 0, taken, plain[:, 128 * j : 128 * j + 128])
    across = [
        jnp.broadcast_to(strip[0:1, 128 * j : 128 * j + 128], (128, 128)).astype(jnp.bfloat16)
        for j in range(TILES)
    ]
    code = jnp.where(lax.broadcasted_iota(jnp.int32, (8, WIDE), 0) == 0, strip[...], 0.0).astype(jnp.bfloat16)
    column = lax.dot_general(
        code, jnp.ones((8, 128), jnp.bfloat16), (((0,), (0,)), ((), ())), preferred_element_type=jnp.float32
    ).astype(jnp.bfloat16)
    for i in range(TILES):
        down = column[128 * i : 128 * i + 128]
        for j in range(TILES):
            mask = compat[128 * i : 128 * i + 128, 128 * j : 128 * j + 128]
            out[0, 128 * i : 128 * i + 128, 128 * j : 128 * j + 128] = jnp.minimum(
                jnp.maximum(across[j] - down, -mask), mask
            )


def payoffs(turn_cards, river_cards, ranks, compat, table):
    smem = pl.BlockSpec(memory_space=pltpu.SMEM)
    vmem = pl.BlockSpec(memory_space=pltpu.VMEM)
    return pl.pallas_call(
        payoff_kernel,
        grid=(4,),
        out_shape=jax.ShapeDtypeStruct((4, WIDE, WIDE), jnp.bfloat16),
        in_specs=[smem] * 2 + [vmem] * 3,
        out_specs=pl.BlockSpec((1, WIDE, WIDE), lambda i: (i, 0, 0)),
        scratch_shapes=[pltpu.VMEM((8, 1408), jnp.float32), pltpu.VMEM((8, WIDE), jnp.float32)],
        compiler_params=pltpu.CompilerParams(vmem_limit_bytes=SMALL_LIMIT),
        cost_estimate=pl.CostEstimate(flops=4 * 4 * WIDE * WIDE, bytes_accessed=10 * WIDE * WIDE, transcendentals=0),
        name="payoff",
    )(turn_cards, river_cards, ranks, compat, table)


def split(value):
    upper = value.astype(jnp.bfloat16)
    return upper, (value - upper.astype(jnp.float32)).astype(jnp.bfloat16)


def split_blocks(blocks, rows):
    lane = lanes_of((8, 128))
    below = 16 * len(blocks)
    for i, block in enumerate(blocks):
        for j in range(TILES):
            if j < 8:
                pair = [block[0, j], block[0, 8 + j]]
            else:
                tails = block[0, 16]
                pair = [jnp.where(lane < 64, v, 0.0) for v in (tails, pltpu.roll(tails, 64, 1))]
            upper, lower = split(jnp.concatenate(pair, axis=0))
            rows[16 * i : 16 * i + 16, 128 * j : 128 * j + 128] = upper
            rows[below + 16 * i : below + 16 * i + 16, 128 * j : 128 * j + 128] = lower


def early_kernel(payoff, select, *rest):
    blocks, (out, rows) = rest[:-2], rest[-2:]
    rl = pl.program_id(0)
    split_blocks(blocks, rows)
    below = 16 * len(blocks)
    parts = [
        jnp.dot(select[...], rows[begin : begin + below], preferred_element_type=jnp.float32).astype(jnp.bfloat16)
        for begin in (0, below)
    ]
    value = jnp.dot(jnp.concatenate(parts, axis=0), payoff[rl], preferred_element_type=jnp.float32)
    out[0] = value[:128] + value[128:]


def early_values(payoff, select, blocks):
    vmem = pl.BlockSpec(memory_space=pltpu.VMEM)
    rows = 16 * len(blocks)
    return pl.pallas_call(
        early_kernel,
        grid=(4,),
        out_shape=jax.ShapeDtypeStruct((4, 128, WIDE), jnp.float32),
        in_specs=[vmem] * 2 + [pl.BlockSpec((1, ROWS, 8, 128), lambda i: (i, 0, 0, 0))] * len(blocks),
        out_specs=pl.BlockSpec((1, 128, WIDE), lambda i: (i, 0, 0)),
        scratch_shapes=[pltpu.VMEM((2 * rows, WIDE), jnp.bfloat16)],
        compiler_params=pltpu.CompilerParams(vmem_limit_bytes=SMALL_LIMIT),
        cost_estimate=pl.CostEstimate(
            flops=4 * 2 * 256 * WIDE * WIDE, bytes_accessed=8 * WIDE * WIDE, transcendentals=0
        ),
        name="early",
    )(payoff, select, *blocks)


def reply_kernel(turn_card, river_card, payoff, early, select, scale, table, *rest):
    blocks, (out, rows) = rest[:-2], rest[-2:]
    t = turn_card[0]
    me = lax.axis_index("hist")
    lane = lanes_of((8, 128))
    rl = pl.program_id(0)

    @pl.when(rl == 0)
    def _():
        out[...] = jnp.zeros_like(out)

    r = river_card[0, 4 * me + rl]
    split_blocks(blocks, rows)
    below = 16 * len(blocks)
    home = home_slots(lane, t, r)
    home_tile, home_lane = home >> 7, home & 127
    first = [jnp.zeros((8, 128), jnp.float32)] * 8
    for start in range(0, WIDE, CHUNK):
        late = jnp.dot(rows[...], payoff[rl, :, start : start + CHUNK], preferred_element_type=jnp.float32)
        parts = jnp.concatenate(split(late[:below] + late[below:]), axis=0)
        value = jnp.dot(select[...], parts, preferred_element_type=jnp.float32)
        value = (value + early[rl, :, start : start + CHUNK]) * scale[...]
        reply = jnp.maximum(value[:64], value[64:])
        for j in range(start // 128, min(start + CHUNK, WIDE) // 128):
            moved = source_lanes(*cards_of(table, j), t, r) >= 0
            for g in range(8):
                part = reply[8 * g : 8 * g + 8, 128 * j - start : 128 * j - start + 128]
                out[g, 1 + j] += jnp.where(moved, 0.0, part)
                first[g] = jnp.where(home_tile == j, pick(part, home_lane), first[g])
    for g in range(8):
        out[g, 0] += first[g]


def replies(turn_cards, river_cards, payoff, early, select, scale, table, blocks):
    smem = pl.BlockSpec(memory_space=pltpu.SMEM)
    vmem = pl.BlockSpec(memory_space=pltpu.VMEM)
    rows = 16 * len(blocks)
    return pl.pallas_call(
        reply_kernel,
        grid=(4,),
        out_shape=jax.ShapeDtypeStruct((8, TILES + 1, 8, 128), jnp.float32),
        in_specs=[smem] * 2
        + [vmem] * 5
        + [pl.BlockSpec((1, ROWS, 8, 128), lambda i: (i, 0, 0, 0))] * len(blocks),
        out_specs=vmem,
        scratch_shapes=[pltpu.VMEM((2 * rows, WIDE), jnp.bfloat16)],
        compiler_params=pltpu.CompilerParams(vmem_limit_bytes=SMALL_LIMIT),
        cost_estimate=pl.CostEstimate(
            flops=4 * 2 * 256 * WIDE * WIDE, bytes_accessed=8 * WIDE * WIDE, transcendentals=0
        ),
        name="reply",
    )(turn_cards, river_cards, payoff, early, select, scale, table, *blocks)


def flat(nodes):
    rows = jnp.transpose(nodes, (0, 2, 1, 3)).reshape(64, TILES + 1, 128)
    body = rows[:, 1:].reshape(64, WIDE)[:, :SLOTS]
    return jnp.concatenate([jnp.zeros((64, LOW), jnp.float32), rows[:, 0, :95], body], axis=1).reshape(-1)


def turn_sum(value, size):
    pairs = [(i, i ^ 1) for i in range(size)]
    half = value.shape[0] // 2
    core = lax.axis_index("turn") & 1
    keep = lax.dynamic_slice_in_dim(value, core * half, half, 0)
    give = lax.dynamic_slice_in_dim(value, (1 - core) * half, half, 0)
    total = keep + lax.ppermute(give, "turn", pairs)
    step = 2
    while step < size:
        for flip in (1, 3):
            total = total + lax.ppermute(total, "turn", [(i, i ^ (flip * step)) for i in range(size)])
        step *= 4
    return total, pairs, core


def per_device(flop_reach, turn_policy, river_policy, hand_rank, turn_cards, river_cards, children, pot):
    groups = lax.axis_size("hist")
    turns = lax.axis_size("turn")
    me = lax.axis_index("hist")
    table = jnp.asarray(np.stack(slot_cards()))
    compat = jnp.asarray(compat_table(), jnp.bfloat16)
    policy = river_policy.reshape(5304, 128)
    common = (turn_cards, river_cards, policy, jnp.transpose(flop_reach), jnp.transpose(turn_policy[0]), table)

    def send(block, s):
        return lax.ppermute(block, "hist", [(i, (i + s) % groups) for i in range(groups)])

    got = {}

    def exchange(shifts, after):
        for s, block in zip(shifts, pack(shifts, *common, after)):
            got[s] = send(block, s) if s else block
        return [got[s] for s in shifts]

    first = exchange((2, 6), [])
    exchange((3, 5), [])
    exchange((4, 1, 7, 0), [])
    payoff = payoffs(turn_cards, river_cards, hand_rank[0], compat, table)
    child = jnp.transpose(children).reshape(128)
    turn_of = jnp.zeros((8,), jnp.int32).at[jnp.array(ORDER)].set(jnp.arange(8, dtype=jnp.int32))
    place = (turn_of[(me - (child >> 4)) & 7] << 4) + ((child & 1) << 3) + ((child >> 1) & 7)
    select = (place[:, None] == jnp.arange(128)[None, :]).astype(jnp.bfloat16)
    scale = jnp.sum(
        jnp.where(child[:, None] == jnp.arange(128)[None, :], pot.astype(jnp.float32)[None, :], 0.0),
        axis=1,
        keepdims=True,
    )
    early = early_values(payoff, select[:, : 16 * EARLY], [got[s] for s in ORDER[:EARLY]])
    late = [got[s] for s in ORDER[EARLY:]]
    twice = jnp.concatenate([select[:, 16 * EARLY :]] * 2, axis=1)
    partial = replies(turn_cards, river_cards, payoff, early, twice, scale, table, late)
    arrived = lax.all_to_all(partial, "hist", 0, 0, tiled=True)
    value = jnp.sum(arrived, axis=0) * (1.0 / 32.0)
    half, pairs, core = turn_sum(value, turns)
    both = jnp.concatenate([value, half * (1.0 / turns)], axis=0)
    spread = lax.all_to_all(jnp.broadcast_to(both, (groups,) + both.shape), "hist", 0, 0, tiled=True)
    here = spread[:, TILES + 1 :]
    there = lax.ppermute(here, "turn", pairs)
    mean = jnp.concatenate([jnp.where(core == 0, here, there), jnp.where(core == 0, there, here)], axis=1)
    return (flat(spread[:, : TILES + 1]).reshape(1, -1), flat(mean))


def solution(mesh):
    return jax.shard_map(
        per_device,
        mesh=mesh,
        in_specs=(
            P(None, "hist"),
            P("turn", None, "hist"),
            P("turn", "hist"),
            P("turn", "hist", None),
            P("turn"),
            P("turn", None),
            P(),
            P(),
        ),
        out_specs=(P("turn", None), P()),
        check_vma=False,
    )
```
